32 devices in a mesh: tok: 8 (over y, x, core), rep: 4 (over z).
Axes of the slice: x: 2, y: 2, z: 4, core: 2. Of those that a mesh axis runs over, the one named last changes fastest.
Arguments:
- hidden_states: bfloat16 [4, 1024, 2048], P('rep', 'tok'), may hold values from -6 to 6
- routes: int32 [4, 1024, 8], P('rep', 'tok'), may hold values from 0 to 31, all different within a row; in each aligned block of 128 rows (0 to 127, 128 to 255, ..., all dimensions but the last counted through in order) at most 36 rows name the same one
- gate_prob: float32 [4, 1024, 8], P('rep', 'tok'), may hold values from 0.03 to 0.3
- gate_up: float32 [32, 2048, 2048], P('tok', 'rep'), may hold values from -0.125 to 0.125
- down: float32 [32, 1024, 2048], P('tok', 'rep'), may hold values from -0.1875 to 0.1875
Outputs:
- mixed: bfloat16 [4, 1024, 2048], P('rep', 'tok')
The draws below stay inside these ranges and needn't reach their ends.
Inputs may be any that keep to these rules, and one draw needn't show every extreme that they name: `routes`: each row names 8 different experts. No expert is named by more than 36 rows of one device's 128 tokens, and some expert reaches 36 on some devices.
All inputs are finite; a program needn't handle non-finite values.
Results may differ from the reference program's by a relative error of at most 0.012.
Values may be sent and summed in bfloat16 or wider, within the bound.
A program may use at most 192 MiB of HBM per device.

```python
import math
import jax
import jax.numpy as jnp
import numpy as np
from jax import lax

D = 2048
FF = 1024
EXPERTS = 32
TOPK = 8
TOK_DEV = 128
CAP = 36
TOKENS = 1024
SERVERS = 4
N_TOK = 8
N_REP = 4


def block_levels(stream_key, dims, split, smallest, top_value):
    factor_of = 1.0
    for axis_at, shards_of in split:
        steps = jax.random.uniform(jax.random.fold_in(jax.random.fold_in(stream_key, 6), axis_at), (shards_of,), jnp.float32, smallest / len(split), top_value / len(split))
        factor_of = factor_of * jnp.repeat(jnp.exp(steps), dims[axis_at] // shards_of).reshape((-1,) + (1,) * (len(dims) - 1 - axis_at))
    return factor_of


def routed_block(key, own, number, rows, number_of, top, limit, slope):
    order = jax.random.permutation(key, number_of)
    packed, usual = portions_of(number_of, rows * top, limit, slope, True), portions_of(number_of, rows * top, limit, slope, False)
    places = jnp.arange(number_of)

    def named(sizes, offset_by):
        used = int((sizes > 0).sum())
        fixed = max(1, used // 4)
        passed = fixed + (places - fixed + offset_by * (used - fixed)) % max(1, number_of - fixed)
        return jnp.zeros((number_of,), jnp.int32).at[order[jnp.where(places < fixed, places, passed)]].set(jnp.asarray(sizes, jnp.int32))

    sizes = jnp.where(number % 4 == 0, named(packed, number // 4), named(usual, number - number // 4 - 1))
    mixed = jax.random.permutation(jax.random.fold_in(own, 3), number_of)
    giver, receiver = mixed[0:number_of // 2 * 2:2], mixed[1:number_of // 2 * 2:2]
    margin = jnp.minimum(sizes[giver] - 1, limit - sizes[receiver]) // 2
    margin = jnp.where((giver == order[0]) | (receiver == order[0]) | (sizes[receiver] == 0), 0, jnp.maximum(margin, 0))
    passed = jax.random.randint(jax.random.fold_in(own, 4), (number_of // 2,), 0, 1 << 20) % (margin + 1)
    sizes = sizes.at[giver].add(-passed).at[receiver].add(passed)
    labels = jnp.searchsorted(jnp.cumsum(sizes), jnp.arange(rows * top), side="right").astype(jnp.int32)
    listing = labels.reshape(top, rows).T
    listing = listing[jax.random.permutation(jax.random.fold_in(own, 1), rows)]
    offset_by = jax.random.randint(jax.random.fold_in(own, 2), (rows, 1), 0, top)
    return jnp.take_along_axis(listing, (jnp.arange(top)[None, :] + offset_by) % top, axis=1)


def portions_of(amount, total, bound, slope, full):
    portions = [(1 << 20) // math.isqrt(standing ** slope) + 1 for standing in range(1, amount + 1)]
    largest = bound if full else min(bound, max(-(-total // amount), total * portions[0] // sum(portions)))
    least = 1 if total - largest >= amount - 1 else 0
    given, spare = [largest] + [least] * (amount - 1), total - largest - least * (amount - 1)
    while spare > 0:
        movable = [i for i in range(1, amount) if given[i] < largest] or [i for i in range(1, amount) if given[i] < bound]
        mass, budget = sum([portions[i] for i in movable]), spare
        for i in movable:
            more = min(bound - given[i], max(1, budget * portions[i] // mass), spare)
            given[i] = given[i] + more
            spare = spare - more
    return np.array(given)


def noise(stream_key, extent, scale, bound, shards=(), kind=jnp.bfloat16):
    array = scale * jax.random.normal(stream_key, extent, jnp.float32)
    if shards:
        array = array * block_levels(stream_key, extent, shards, -0.22, 0.18)
    return jnp.clip(array, -bound, bound).astype(kind)


def setup_inputs(seed: int = 0) -> dict:
    seeds = jax.random.split(jax.random.key(seed), 6)
    hidden_states = noise(seeds[0], (SERVERS, TOKENS, D), 1.0, 6.0, ((0, 4), (1, 8)))
    routes_keys = jax.random.split(jax.random.fold_in(seeds[1], 1), SERVERS * TOKENS // TOK_DEV)
    routes_turns = jax.random.permutation(jax.random.fold_in(seeds[1], 3), SERVERS * TOKENS // TOK_DEV)
    routes = jax.vmap(lambda own, number: routed_block(jax.random.fold_in(seeds[1], 2), own, number, TOK_DEV, EXPERTS, TOPK, CAP, 1))(routes_keys, routes_turns).reshape((SERVERS, TOKENS, TOPK))
    gate_prob = jnp.clip(jnp.exp(math.log(0.3) - 2.3025852 * jax.random.uniform(seeds[2], (SERVERS, TOKENS, TOPK), jnp.float32) ** block_levels(seeds[2], (SERVERS, TOKENS, TOPK), ((0, 4), (1, 8)), -0.2, 0.2)), 0.03, 0.3)
    gate_up = noise(seeds[3], (EXPERTS, D, 2 * FF), D ** -0.5, 0.125, ((0, 8), (1, 4)), jnp.float32)
    down = noise(seeds[4], (EXPERTS, FF, D), FF ** -0.5, 0.1875, ((0, 8), (1, 4)), jnp.float32)
    return dict(hidden_states=hidden_states, routes=routes, gate_prob=gate_prob, gate_up=gate_up, down=down)


def reference(hidden_states, routes, gate_prob, gate_up, down):
    served_gate_up = gate_up.astype(jnp.bfloat16)
    served_down = down.astype(jnp.bfloat16)
    flat_rows = hidden_states.reshape(-1, D)
    flat_picks = routes.reshape(-1).astype(jnp.int32)
    flat_probs = gate_prob.reshape(-1)
    pick_count = flat_picks.shape[0]
    owners = (jnp.arange(pick_count, dtype=jnp.int32) // TOPK).astype(jnp.int32)
    most_rows = N_REP * N_TOK * CAP

    def one_expert(running, expert):
        chosen = jnp.nonzero(flat_picks == expert, size=most_rows, fill_value=pick_count)[0].astype(jnp.int32)
        usable = chosen < pick_count
        safe_index = jnp.where(usable, chosen, 0).astype(jnp.int32)
        token_index = owners[safe_index]
        rows = flat_rows[token_index]
        both_parts = jnp.dot(rows, served_gate_up[expert], preferred_element_type=jnp.float32)
        units = (jax.nn.silu(both_parts[:, :FF]) * both_parts[:, FF:]).astype(jnp.bfloat16)
        expert_out = jnp.dot(units, served_down[expert], preferred_element_type=jnp.float32).astype(jnp.bfloat16)
        weights = jnp.where(usable, flat_probs[safe_index], jnp.float32(0.0))
        weighted = expert_out.astype(jnp.float32) * weights[:, None]
        running = running.at[token_index].add(weighted)
        return running, None

    start_sum = jnp.zeros((flat_rows.shape[0], D), jnp.float32)
    total, unused_out = lax.scan(one_expert, start_sum, jnp.arange(EXPERTS, dtype=jnp.int32))
    return total.astype(jnp.bfloat16).reshape(hidden_states.shape)
```

```python
import jax
import jax.numpy as jnp
from jax import lax
from jax.sharding import PartitionSpec as P

GATHER_BYTES = 16 << 20


def reshard_gate_up(gate_up, reps):
    experts, rows, columns = gate_up.shape
    part = columns // 2 // reps
    me = lax.axis_index("rep")
    pieces = (
        gate_up.astype(jnp.bfloat16)
        .reshape(experts, rows, 2, reps, part)
        .transpose(3, 2, 1, 0, 4)
        .reshape(reps, 2, rows, experts * part)
    )
    whole = jnp.zeros((2, reps, rows, experts * part), jnp.bfloat16)
    for shift in range(reps):
        piece = lax.dynamic_index_in_dim(pieces, lax.rem(me + shift, reps), 0, keepdims=False)
        if shift:
            piece = lax.ppermute(piece, "rep", [(i, (i + shift) % reps) for i in range(reps)])
        source = lax.rem(me + reps - shift, reps)
        whole = lax.dynamic_update_slice(whole, piece[:, None], (0, source, 0, 0))
    whole = whole.reshape(2, reps * rows, experts * part)
    return whole[0], whole[1]


def per_device(hidden_states, routes, gate_prob, gate_up, down):
    groups = lax.axis_size("tok")
    reps = lax.axis_size("rep")
    experts = gate_up.shape[0]
    _, token_count, width = hidden_states.shape
    part = gate_up.shape[2] // 2 // reps
    all_experts = groups * experts
    tokens = hidden_states[0]
    total_bytes = groups * reps * token_count * width * 2
    chunks = max(1, total_bytes // GATHER_BYTES)
    chunk = token_count // chunks

    hit = routes[0][:, :, None] == jnp.arange(all_experts, dtype=jnp.int32)
    weight = jnp.sum(jnp.where(hit, gate_prob[0][:, :, None], 0.0), axis=1)
    gate, up = reshard_gate_up(gate_up, reps)
    stacked_down = down.astype(jnp.bfloat16).reshape(experts * part, width)
    first = lax.axis_index("tok") * experts

    def one_chunk(rows, row_weight):
        everyone = lax.all_gather(rows, ("rep", "tok"), axis=0, tiled=True)
        all_weight = lax.all_gather(row_weight, ("rep", "tok"), axis=0, tiled=True)
        mine = lax.dynamic_slice_in_dim(all_weight, first, experts, 1)
        scale = jnp.repeat(mine, part, axis=1)
        g = jnp.dot(everyone, gate, preferred_element_type=jnp.float32)
        u = jnp.dot(everyone, up, preferred_element_type=jnp.float32)
        units = (jax.nn.silu(g) * u * scale).astype(jnp.bfloat16)
        partial = jnp.dot(units, stacked_down, preferred_element_type=jnp.float32)
        return lax.psum_scatter(
            partial.astype(jnp.bfloat16), ("rep", "tok"), scatter_dimension=0, tiled=True
        )

    if chunks == 1:
        return one_chunk(tokens, weight)[None]
    mixed = lax.map(
        lambda part_of: one_chunk(*part_of),
        (tokens.reshape(chunks, chunk, width), weight.reshape(chunks, chunk, all_experts)),
    )
    return mixed.reshape(1, token_count, width)


def solution(mesh):
    return jax.shard_map(
        per_device,
        mesh=mesh,
        in_specs=(
            P("rep", "tok", None),
            P("rep", "tok", None),
            P("rep", "tok", None),
            P("tok", "rep", None),
            P("tok", "rep", None),
        ),
        out_specs=P("rep", "tok", None),
        check_vma=False,
    )
```

```python
import jax
import jax.numpy as jnp
from jax import lax
from jax.experimental import pallas as pl
from jax.experimental.pallas import tpu as pltpu
from jax.sharding import PartitionSpec as P

GATHER_BYTES = 16 << 20


def reshard_gate_up(gate_up, reps):
    experts, rows, columns = gate_up.shape
    part = columns // 2 // reps
    me = lax.axis_index("rep")
    pieces = (
        gate_up.astype(jnp.bfloat16)
        .reshape(experts, rows, 2, reps, part)
        .transpose(3, 2, 1, 0, 4)
        .reshape(reps, 2, rows, experts * part)
    )
    whole = jnp.zeros((2, reps, rows, experts * part), jnp.bfloat16)
    for shift in range(reps):
        piece = lax.dynamic_index_in_dim(pieces, lax.rem(me + shift, reps), 0, keepdims=False)
        if shift:
            piece = lax.ppermute(piece, "rep", [(i, (i + shift) % reps) for i in range(reps)])
        source = lax.rem(me + reps - shift, reps)
        whole = lax.dynamic_update_slice(whole, piece[:, None], (0, source, 0, 0))
    whole = whole.reshape(2, reps * rows, experts * part)
    return whole[0], whole[1]


LANES = 128
HALVES = 2


def fused_kernel(
    x_ref, sel_ref, gate_ref, down_ref, out_ref,
    x, w, d, units, r1, r2, r3, rz,
    local_sem, w_send, w_recv, z_send, z_recv, ag_send, ag_recv, rs_send, rs_recv, o_send, o_recv,
):
    reps, _, _, _, rows, _ = x.shape
    experts, depth, both = w.shape
    part = both // 2
    width = d.shape[1]
    block_depth = depth // reps
    ff = gate_ref.shape[2] // 2
    r = lax.axis_index("rep")
    t = lax.axis_index("tok")
    core = lax.rem(t, 2)
    xs = lax.rem(lax.div(t, 2), 2)
    ys = lax.div(t, 4)
    core_mate = {"tok": t + 1 - 2 * core}
    x_mate = {"tok": t + 2 - 4 * xs}
    y_mate = {"tok": t + 4 - 8 * ys}
    rep_mates = [{"rep": lax.rem(r + k, reps)} for k in range(1, reps)]
    other = 1 - core

    barrier = pltpu.get_barrier_semaphore()
    mates = [core_mate, x_mate, y_mate] + rep_mates
    for mate in mates:
        pl.semaphore_signal(barrier, inc=1, device_id=mate, device_id_type=pl.DeviceIdType.MESH)
    pl.semaphore_wait(barrier, len(mates))

    def remote(src, dst, send, recv, mate):
        copy = pltpu.make_async_remote_copy(
            src_ref=src, dst_ref=dst, send_sem=send, recv_sem=recv,
            device_id=mate, device_id_type=pl.DeviceIdType.MESH,
        )
        copy.start()
        return copy

    def local(src, dst, sem):
        copy = pltpu.make_async_copy(src, dst, sem)
        copy.start()
        return copy

    own_x = local(x_ref, x.at[r, ys, xs, core], local_sem.at[0])
    to_reps = [
        remote(x_ref, x.at[r, ys, xs, core], z_send.at[k], z_recv.at[k], rep_mates[k])
        for k in range(reps - 1)
    ]
    landing = pl.ds(pl.multiple_of(r * block_depth, block_depth), block_depth)

    def send_weights(e):
        copies = []
        for half in range(HALVES):
            into = w.at[e, landing, pl.ds(half * part, part)]
            for k in range(1, reps):
                to = lax.rem(r + k, reps)
                columns = pl.ds(pl.multiple_of(half * ff + to * part, part), part)
                copies.append(
                    remote(
                        gate_ref.at[e, :, columns], into,
                        w_send.at[e, k - 1, half], w_recv.at[e, k - 1, half], rep_mates[k - 1],
                    )
                )
            columns = pl.ds(pl.multiple_of(half * ff + r * part, part), part)
            copies.append(
                local(gate_ref.at[e, :, columns], into, local_sem.at[2 + HALVES * e + half])
            )
        return copies

    weights = [send_weights(e) for e in range(experts - 1)]
    own_d = local(down_ref, d, local_sem.at[1])

    own_x.wait()
    chunk_of = [lax.rem(r + reps - i, reps) for i in range(reps)]
    stage = []
    for i in range(reps):
        if i:
            to_reps[i - 1].wait()
        mine = x.at[chunk_of[i], ys, xs, core]
        mate = x_mate if i % 2 == 0 else y_mate
        stage.append(remote(mine, mine, ag_send.at[i, 0], ag_recv.at[i, 0], mate))
    for i in range(reps):
        stage[i].wait()
        if i % 2 == 0:
            mine, mate = x.at[chunk_of[i], ys, :, core], y_mate
        else:
            mine, mate = x.at[chunk_of[i], :, xs, core], x_mate
        stage[i] = remote(mine, mine, ag_send.at[i, 1], ag_recv.at[i, 1], mate)
    for i in range(reps):
        stage[i].wait()
        mine = x.at[chunk_of[i], :, :, core]
        stage[i] = remote(mine, mine, ag_send.at[i, 2], ag_recv.at[i, 2], core_mate)
    weights.append(send_weights(experts - 1))
    for i in range(reps):
        stage[i].wait()

    def make_units(e, i, half):
        c = lax.rem(r + 1 + i, reps)
        h = other + half * (core - other)
        values = x[c, :, :, h, :, pl.ds(0, width)].reshape(4 * rows, width)
        marks = x[c, :, :, h, :, pl.ds(width, LANES)].reshape(4 * rows, LANES)
        y = jnp.dot(values, w[e], preferred_element_type=jnp.float32)
        scale = jnp.dot(marks, sel_ref[e], preferred_element_type=jnp.float32)
        g, u = y[:, :part], y[:, part:]
        unit = g * (1.0 / (1.0 + jnp.exp(-g))) * u * scale
        units[i, half, :, pl.ds(e * part, part)] = unit.astype(jnp.bfloat16)

    def project(i, half):
        c = lax.rem(r + 1 + i, reps)
        h = other if half == 0 else core
        step = 512

        def columns_of(n, carry):
            columns = pl.ds(pl.multiple_of(n * step, step), step)
            total = jnp.dot(units[i, half], d[:, columns], preferred_element_type=jnp.float32)
            total = total.reshape(2, 2, rows, step)
            if half:
                total = total + r1[i, :, :, :, columns].astype(jnp.float32)
            x[c, :, :, h, :, columns] = total.astype(jnp.bfloat16)
            return carry

        lax.fori_loop(0, width // step, columns_of, 0)

    for e in range(experts - 1):
        for copy in weights[e]:
            copy.wait()

        def tile(n, carry):
            make_units(e, lax.div(n, 2), lax.rem(n, 2))
            return carry

        lax.fori_loop(0, 2 * reps, tile, 0)
    for copy in weights[experts - 1]:
        copy.wait()
    own_d.wait()

    flat = pl.ds(0, width)
    first, second, third, last = {}, {}, {}, []

    def scatter_core(i):
        make_units(experts - 1, i, 0)
        project(i, 0)
        c = lax.rem(r + 1 + i, reps)
        first[i] = remote(
            x.at[c, :, :, other, :, flat], r1.at[i], rs_send.at[i, 0], rs_recv.at[i, 0], core_mate
        )

    def scatter_second(i):
        make_units(experts - 1, i, 1)
        first[i].wait_recv()
        project(i, 1)
        c = lax.rem(r + 1 + i, reps)
        if i % 2 == 0:
            src, mate = x.at[c, :, 1 - xs, core, :, flat], x_mate
        else:
            src, mate = x.at[c, 1 - ys, :, core, :, flat], y_mate
        second[i] = remote(src, r2.at[i], rs_send.at[i, 1], rs_recv.at[i, 1], mate)

    def scatter_third(i):
        second[i].wait_recv()
        c = lax.rem(r + 1 + i, reps)

        def add(n, carry):
            at = pl.ds(pl.multiple_of(n * 16, 16), 16)
            for k in range(2):
                where = (c, k, xs, core, at, flat) if i % 2 == 0 else (c, ys, k, core, at, flat)
                total = x[where].astype(jnp.float32) + r2[i, k, at, :].astype(jnp.float32)
                x[where] = total.astype(jnp.bfloat16)
            return carry

        lax.fori_loop(0, rows // 16, add, 0)
        if i % 2 == 0:
            src, mate = x.at[c, 1 - ys, xs, core, :, flat], y_mate
        else:
            src, mate = x.at[c, ys, 1 - xs, core, :, flat], x_mate
        third[i] = remote(src, r3.at[i], rs_send.at[i, 2], rs_recv.at[i, 2], mate)

    def scatter_rep(i):
        third[i].wait_recv()
        c = lax.rem(r + 1 + i, reps)
        if i == reps - 1:
            return

        def add(n, carry):
            at = pl.ds(pl.multiple_of(n * 16, 16), 16)
            where = (c, ys, xs, core, at, flat)
            total = x[where].astype(jnp.float32) + r3[i, at, :].astype(jnp.float32)
            x[where] = total.astype(jnp.bfloat16)
            return carry

        lax.fori_loop(0, rows // 16, add, 0)
        last.append(
            remote(
                x.at[c, ys, xs, core, :, flat], rz.at[i], o_send.at[i], o_recv.at[i], rep_mates[i]
            )
        )

    for step in range(reps + 3):
        if step < reps:
            scatter_core(step)
        for lag, work in ((1, scatter_second), (2, scatter_third), (3, scatter_rep)):
            if 0 <= step - lag < reps:
                work(step - lag)
    for copy in last:
        copy.wait_recv()

    def finish(n, carry):
        at = pl.ds(pl.multiple_of(n * 16, 16), 16)
        total = x[r, ys, xs, core, at, flat].astype(jnp.float32)
        total = total + r3[reps - 1, at, :].astype(jnp.float32)
        for k in range(reps - 1):
            total = total + rz[k, at, :].astype(jnp.float32)
        out_ref[at, :] = total.astype(jnp.bfloat16)
        return carry

    lax.fori_loop(0, rows // 16, finish, 0)
    for copy in list(first.values()) + list(second.values()) + list(third.values()) + last:
        copy.wait_send()


def fused(tokens, weight, gate_up, down, reps):
    rows, width = tokens.shape
    experts, block_depth, columns = gate_up.shape
    part = columns // 2 // reps
    all_experts = weight.shape[1]
    high = lax.reduce_precision(weight, 8, 7)
    marks = jnp.concatenate([high, weight - high], axis=1).astype(jnp.bfloat16)
    marks = jnp.pad(marks, ((0, 0), (0, LANES - 2 * all_experts)))
    x = jnp.concatenate([tokens, marks], axis=1)
    lane = jnp.arange(LANES, dtype=jnp.int32)
    own = lax.axis_index("tok") * experts + jnp.arange(experts, dtype=jnp.int32)
    chosen = (lane[None, :] == own[:, None]) | (lane[None, :] == own[:, None] + all_experts)
    sel = jnp.broadcast_to(chosen[:, :, None], (experts, LANES, part)).astype(jnp.bfloat16)
    depth = block_depth * reps
    bf16 = jnp.bfloat16
    dma = pltpu.SemaphoreType.DMA
    hbm = pl.BlockSpec(memory_space=pl.ANY)
    vmem = pl.BlockSpec(memory_space=pltpu.VMEM)
    return pl.pallas_call(
        fused_kernel,
        out_shape=jax.ShapeDtypeStruct((rows, width), bf16),
        in_specs=[hbm, vmem, hbm, hbm],
        out_specs=vmem,
        scratch_shapes=[
            pltpu.VMEM((reps, 2, 2, 2, rows, width + LANES), bf16),
            pltpu.VMEM((experts, depth, 2 * part), bf16),
            pltpu.VMEM((experts * part, width), bf16),
            pltpu.VMEM((reps, 2, 4 * rows, experts * part), bf16),
            pltpu.VMEM((reps, 2, 2, rows, width), bf16),
            pltpu.VMEM((reps, 2, rows, width), bf16),
            pltpu.VMEM((reps, rows, width), bf16),
            pltpu.VMEM((reps - 1, rows, width), bf16),
            dma((2 + HALVES * experts,)),
            dma((experts, reps - 1, HALVES)),
            dma((experts, reps - 1, HALVES)),
            dma((reps - 1,)),
            dma((reps - 1,)),
            dma((reps, 3)),
            dma((reps, 3)),
            dma((reps, 3)),
            dma((reps, 3)),
            dma((reps - 1,)),
            dma((reps - 1,)),
        ],
        compiler_params=pltpu.CompilerParams(
            collective_id=0, has_side_effects=True, vmem_limit_bytes=62 << 20
        ),
    )(x, sel, gate_up.astype(bf16), down.astype(bf16).reshape(experts * part, width))


def per_device(hidden_states, routes, gate_prob, gate_up, down):
    groups = lax.axis_size("tok")
    reps = lax.axis_size("rep")
    experts = gate_up.shape[0]
    _, token_count, width = hidden_states.shape
    part = gate_up.shape[2] // 2 // reps
    all_experts = groups * experts
    tokens = hidden_states[0]
    total_bytes = groups * reps * token_count * width * 2
    chunks = max(1, total_bytes // GATHER_BYTES)
    chunk = token_count // chunks

    hit = routes[0][:, :, None] == jnp.arange(all_experts, dtype=jnp.int32)
    weight = jnp.sum(jnp.where(hit, gate_prob[0][:, :, None], 0.0), axis=1)
    if chunks == 1 and groups == 8 and reps == 4 and 2 * all_experts <= LANES:
        return fused(tokens, weight, gate_up, down, reps)[None]
    gate, up = reshard_gate_up(gate_up, reps)
    stacked_down = down.astype(jnp.bfloat16).reshape(experts * part, width)
    first = lax.axis_index("tok") * experts

    def one_chunk(rows, row_weight):
        everyone = lax.all_gather(rows, ("rep", "tok"), axis=0, tiled=True)
        all_weight = lax.all_gather(row_weight, ("rep", "tok"), axis=0, tiled=True)
        mine = lax.dynamic_slice_in_dim(all_weight, first, experts, 1)
        scale = jnp.repeat(mine, part, axis=1)
        g = jnp.dot(everyone, gate, preferred_element_type=jnp.float32)
        u = jnp.dot(everyone, up, preferred_element_type=jnp.float32)
        units = (jax.nn.silu(g) * u * scale).astype(jnp.bfloat16)
        partial = jnp.dot(units, stacked_down, preferred_element_type=jnp.float32)
        return lax.psum_scatter(
            partial.astype(jnp.bfloat16), ("rep", "tok"), scatter_dimension=0, tiled=True
        )

    if chunks == 1:
        return one_chunk(tokens, weight)[None]
    mixed = lax.map(
        lambda part_of: one_chunk(*part_of),
        (tokens.reshape(chunks, chunk, width), weight.reshape(chunks, chunk, all_experts)),
    )
    return mixed.reshape(1, token_count, width)


def solution(mesh):
    return jax.shard_map(
        per_device,
        mesh=mesh,
        in_specs=(
            P("rep", "tok", None),
            P("rep", "tok", None),
            P("rep", "tok", None),
            P("tok", "rep", None),
            P("tok", "rep", None),
        ),
        out_specs=P("rep", "tok", None),
        check_vma=False,
    )
```

```python
import jax
import jax.numpy as jnp
from jax import lax
from jax.experimental import pallas as pl
from jax.experimental.pallas import tpu as pltpu
from jax.sharding import PartitionSpec as P

GATHER_BYTES = 16 << 20


def reshard_gate_up(gate_up, reps):
    experts, rows, columns = gate_up.shape
    part = columns // 2 // reps
    me = lax.axis_index("rep")
    pieces = (
        gate_up.astype(jnp.bfloat16)
        .reshape(experts, rows, 2, reps, part)
        .transpose(3, 2, 1, 0, 4)
        .reshape(reps, 2, rows, experts * part)
    )
    whole = jnp.zeros((2, reps, rows, experts * part), jnp.bfloat16)
    for shift in range(reps):
        piece = lax.dynamic_index_in_dim(pieces, lax.rem(me + shift, reps), 0, keepdims=False)
        if shift:
            piece = lax.ppermute(piece, "rep", [(i, (i + shift) % reps) for i in range(reps)])
        source = lax.rem(me + reps - shift, reps)
        whole = lax.dynamic_update_slice(whole, piece[:, None], (0, source, 0, 0))
    whole = whole.reshape(2, reps * rows, experts * part)
    return whole[0], whole[1]


LANES = 128
HALVES = 2


def fused_kernel(
    x_ref, sel_ref, gate_ref, down_ref, out_ref, served,
    x, w, d, units, r1, r2, r3, rz, wide, narrow,
    local_sem, load_sem, store_sem, w_send, w_recv, z_send, z_recv, ag_send, ag_recv, rs_send, rs_recv, o_send, o_recv,
):
    reps, _, _, _, rows, _ = x.shape
    experts, depth, both = w.shape
    part = both // 2
    width = d.shape[1]
    block_depth = depth // reps
    ff = gate_ref.shape[2] // 2
    r = lax.axis_index("rep")
    t = lax.axis_index("tok")
    core = lax.rem(t, 2)
    xs = lax.rem(lax.div(t, 2), 2)
    ys = lax.div(t, 4)
    core_mate = {"tok": t + 1 - 2 * core}
    x_mate = {"tok": t + 2 - 4 * xs}
    y_mate = {"tok": t + 4 - 8 * ys}
    rep_mates = [{"rep": lax.rem(r + k, reps)} for k in range(1, reps)]
    across = reps - 1 - r
    beside = r + 1 - 2 * lax.rem(r, 2)
    piece = wide.shape[1]
    other = 1 - core

    barrier = pltpu.get_barrier_semaphore()
    mates = [core_mate, x_mate, y_mate] + rep_mates
    for mate in mates:
        pl.semaphore_signal(barrier, inc=1, device_id=mate, device_id_type=pl.DeviceIdType.MESH)
    pl.semaphore_wait(barrier, len(mates))

    def remote(src, dst, send, recv, mate):
        copy = pltpu.make_async_remote_copy(
            src_ref=src, dst_ref=dst, send_sem=send, recv_sem=recv,
            device_id=mate, device_id_type=pl.DeviceIdType.MESH,
        )
        copy.start()
        return copy

    def local(src, dst, sem):
        copy = pltpu.make_async_copy(src, dst, sem)
        copy.start()
        return copy

    mine = x.at[r, ys, xs, core]
    own_x = local(x_ref, mine, local_sem.at[0])
    from_across = remote(x_ref, mine, z_send.at[0], z_recv.at[0], {"rep": across})
    from_beside = remote(x_ref, mine, z_send.at[1], z_recv.at[1], {"rep": beside})

    def cast_rows(src, dst_store):
        def some(n, carry):
            at = pl.ds(pl.multiple_of(n * 16, 16), 16)
            dst_store(at, n, src[at, :].astype(jnp.bfloat16))
            return carry

        lax.fori_loop(0, piece // 16, some, 0)

    def load(source, n):
        rows_of = pl.ds(n * piece, piece)
        return local(source.at[rows_of, :], wide.at[n % 2], load_sem.at[n % 2])

    def cast_expert(e):
        count = gate_ref.shape[1] // piece
        loads, stores = [load(gate_ref.at[e], 0)], []
        for n in range(count):
            if n + 1 < count:
                loads.append(load(gate_ref.at[e], n + 1))
            loads[n].wait()
            if n >= 2:
                stores[n - 2].wait()

            def keep(at, step, value, slot=n % 2):
                narrow[slot, at, :] = value

            cast_rows(wide.at[n % 2], keep)
            stores.append(
                local(
                    narrow.at[n % 2], served.at[e, pl.ds(n * piece, piece), :], store_sem.at[n % 2]
                )
            )
        for store in stores[-2:]:
            store.wait()

    def cast_down():
        count = d.shape[0] // piece
        loads = [load(down_ref, 0)]
        for n in range(count):
            if n + 1 < count:
                loads.append(load(down_ref, n + 1))
            loads[n].wait()

            def keep(at, step, value, base=n * piece):
                d[pl.ds(pl.multiple_of(base + step * 16, 16), 16), :] = value

            cast_rows(wide.at[n % 2], keep)

    landing = pl.ds(pl.multiple_of(r * block_depth, block_depth), block_depth)

    def send_weights(e):
        copies = []
        for half in range(HALVES):
            into = w.at[e, landing, pl.ds(half * part, part)]
            for k in range(1, reps):
                to = lax.rem(r + k, reps)
                columns = pl.ds(pl.multiple_of(half * ff + to * part, part), part)
                copies.append(
                    remote(
                        served.at[e, :, columns], into,
                        w_send.at[e, k - 1, half], w_recv.at[e, k - 1, half], rep_mates[k - 1],
                    )
                )
            columns = pl.ds(pl.multiple_of(half * ff + r * part, part), part)
            copies.append(
                local(served.at[e, :, columns], into, local_sem.at[2 + HALVES * e + half])
            )
        return copies

    cast_expert(0)
    weights = [send_weights(0)]

    chunk_of = [r, across, beside, reps - 1 - beside]
    stage = []

    def gather_first(i):
        block = x.at[chunk_of[i], ys, xs, core]
        mate = x_mate if i % 2 == 0 else y_mate
        stage.append(remote(block, block, ag_send.at[i, 0], ag_recv.at[i, 0], mate))

    own_x.wait()
    gather_first(0)
    cast_expert(1)
    from_across.wait()
    block = x.at[across, ys, xs, core]
    forwarded = remote(block, block, z_send.at[2], z_recv.at[2], {"rep": beside})
    gather_first(1)
    from_beside.wait()
    gather_first(2)
    weights.append(send_weights(1))
    forwarded.wait()
    gather_first(3)
    cast_expert(2)
    for i in range(reps):
        stage[i].wait()
        if i % 2 == 0:
            block, mate = x.at[chunk_of[i], ys, :, core], y_mate
        else:
            block, mate = x.at[chunk_of[i], :, xs, core], x_mate
        stage[i] = remote(block, block, ag_send.at[i, 1], ag_recv.at[i, 1], mate)

    def arrive(e):
        for copy in weights[e]:
            copy.wait()
        if e + 2 < experts:
            weights.append(send_weights(e + 2))

    arrive(0)
    for i in range(reps):
        stage[i].wait()
        block = x.at[chunk_of[i], :, :, core]
        stage[i] = remote(block, block, ag_send.at[i, 2], ag_recv.at[i, 2], core_mate)
    cast_expert(3)
    cast_down()
    for i in range(reps):
        stage[i].wait()

    def make_units(e, i, half):
        c = lax.rem(r + 1 + i, reps)
        h = other + half * (core - other)
        values = x[c, :, :, h, :, pl.ds(0, width)].reshape(4 * rows, width)
        marks = x[c, :, :, h, :, pl.ds(width, LANES)].reshape(4 * rows, LANES)
        y = jnp.dot(values, w[e], preferred_element_type=jnp.float32)
        scale = jnp.dot(marks, sel_ref[e], preferred_element_type=jnp.float32)
        g, u = y[:, :part], y[:, part:]
        unit = g * (1.0 / (1.0 + jnp.exp(-g))) * u * scale
        units[i, half, :, pl.ds(e * part, part)] = unit.astype(jnp.bfloat16)

    def project(i, half):
        c = lax.rem(r + 1 + i, reps)
        h = other if half == 0 else core
        step = 512

        def columns_of(n, carry):
            columns = pl.ds(pl.multiple_of(n * step, step), step)
            total = jnp.dot(units[i, half], d[:, columns], preferred_element_type=jnp.float32)
            total = total.reshape(2, 2, rows, step)
            if half:
                total = total + r1[i, :, :, :, columns].astype(jnp.float32)
            x[c, :, :, h, :, columns] = total.astype(jnp.bfloat16)
            return carry

        lax.fori_loop(0, width // step, columns_of, 0)

    for e in range(experts - 1):
        if e:
            arrive(e)

        def tile(n, carry):
            make_units(e, lax.div(n, 2), lax.rem(n, 2))
            return carry

        lax.fori_loop(0, 2 * reps, tile, 0)
    arrive(experts - 1)

    flat = pl.ds(0, width)
    streams = [pl.ds(q * (width // 2), width // 2) for q in range(2)]
    first, second, third, last = {}, {}, {}, []

    def scatter_core(i):
        make_units(experts - 1, i, 0)
        project(i, 0)
        c = lax.rem(r + 1 + i, reps)
        first[i] = remote(
            x.at[c, :, :, other, :, flat], r1.at[i], rs_send.at[i, 0], rs_recv.at[i, 0], core_mate
        )

    def scatter_second(i):
        make_units(experts - 1, i, 1)
        first[i].wait_recv()
        project(i, 1)
        c = lax.rem(r + 1 + i, reps)
        for q, columns in enumerate(streams):
            if q == 0:
                src, mate = x.at[c, :, 1 - xs, core, :, columns], x_mate
            else:
                src, mate = x.at[c, 1 - ys, :, core, :, columns], y_mate
            second[i, q] = remote(
                src, r2.at[i, :, :, columns], rs_send.at[i, 1 + q], rs_recv.at[i, 1 + q], mate
            )

    def scatter_third(i):
        c = lax.rem(r + 1 + i, reps)
        for q, columns in enumerate(streams):
            second[i, q].wait_recv()

            def add(n, carry, q=q, columns=columns):
                at = pl.ds(pl.multiple_of(n * 16, 16), 16)
                for k in range(2):
                    where = (c, k, xs, core, at, columns) if q == 0 else (c, ys, k, core, at, columns)
                    total = x[where].astype(jnp.float32) + r2[i, k, at, columns].astype(jnp.float32)
                    x[where] = total.astype(jnp.bfloat16)
                return carry

            lax.fori_loop(0, rows // 16, add, 0)
            if q == 0:
                src, mate = x.at[c, 1 - ys, xs, core, :, columns], y_mate
            else:
                src, mate = x.at[c, ys, 1 - xs, core, :, columns], x_mate
            third[i, q] = remote(
                src, r3.at[i, :, columns], rs_send.at[i, 3 + q], rs_recv.at[i, 3 + q], mate
            )

    def scatter_rep(i):
        for q in range(2):
            third[i, q].wait_recv()
        c = lax.rem(r + 1 + i, reps)
        if i == reps - 1:
            return

        def add(n, carry):
            at = pl.ds(pl.multiple_of(n * 16, 16), 16)
            where = (c, ys, xs, core, at, flat)
            total = x[where].astype(jnp.float32) + r3[i, at, :].astype(jnp.float32)
            x[where] = total.astype(jnp.bfloat16)
            return carry

        lax.fori_loop(0, rows // 16, add, 0)
        last.append(
            remote(
                x.at[c, ys, xs, core, :, flat], rz.at[i], o_send.at[i], o_recv.at[i], rep_mates[i]
            )
        )

    for step in range(reps + 3):
        if step < reps:
            scatter_core(step)
        for lag, work in ((1, scatter_second), (2, scatter_third), (3, scatter_rep)):
            if 0 <= step - lag < reps:
                work(step - lag)
    for copy in last:
        copy.wait_recv()

    def finish(n, carry):
        at = pl.ds(pl.multiple_of(n * 16, 16), 16)
        total = x[r, ys, xs, core, at, flat].astype(jnp.float32)
        total = total + r3[reps - 1, at, :].astype(jnp.float32)
        for k in range(reps - 1):
            total = total + rz[k, at, :].astype(jnp.float32)
        out_ref[at, :] = total.astype(jnp.bfloat16)
        return carry

    lax.fori_loop(0, rows // 16, finish, 0)
    for copy in list(first.values()) + list(second.values()) + list(third.values()) + last:
        copy.wait_send()


def fused(tokens, weight, gate_up, down, reps):
    rows, width = tokens.shape
    experts, block_depth, columns = gate_up.shape
    part = columns // 2 // reps
    all_experts = weight.shape[1]
    high = lax.reduce_precision(weight, 8, 7)
    marks = jnp.concatenate([high, weight - high], axis=1).astype(jnp.bfloat16)
    marks = jnp.pad(marks, ((0, 0), (0, LANES - 2 * all_experts)))
    x = jnp.concatenate([tokens, marks], axis=1)
    lane = jnp.arange(LANES, dtype=jnp.int32)
    own = lax.axis_index("tok") * experts + jnp.arange(experts, dtype=jnp.int32)
    chosen = (lane[None, :] == own[:, None]) | (lane[None, :] == own[:, None] + all_experts)
    sel = jnp.broadcast_to(chosen[:, :, None], (experts, LANES, part)).astype(jnp.bfloat16)
    depth = block_depth * reps
    bf16 = jnp.bfloat16
    dma = pltpu.SemaphoreType.DMA
    hbm = pl.BlockSpec(memory_space=pl.ANY)
    vmem = pl.BlockSpec(memory_space=pltpu.VMEM)
    return pl.pallas_call(
        fused_kernel,
        out_shape=[
            jax.ShapeDtypeStruct((rows, width), bf16),
            jax.ShapeDtypeStruct(gate_up.shape, bf16),
        ],
        in_specs=[hbm, vmem, hbm, hbm],
        out_specs=[vmem, hbm],
        scratch_shapes=[
            pltpu.VMEM((reps, 2, 2, 2, rows, width + LANES), bf16),
            pltpu.VMEM((experts, depth, 2 * part), bf16),
            pltpu.VMEM((experts * part, width), bf16),
            pltpu.VMEM((reps, 2, 4 * rows, experts * part), bf16),
            pltpu.VMEM((reps, 2, 2, rows, width), bf16),
            pltpu.VMEM((reps, 2, rows, width), bf16),
            pltpu.VMEM((reps, rows, width), bf16),
            pltpu.VMEM((reps - 1, rows, width), bf16),
            pltpu.VMEM((2, 128, columns), jnp.float32),
            pltpu.VMEM((2, 128, columns), bf16),
            dma((2 + HALVES * experts,)),
            dma((2,)),
            dma((2,)),
            dma((experts, reps - 1, HALVES)),
            dma((experts, reps - 1, HALVES)),
            dma((reps - 1,)),
            dma((reps - 1,)),
            dma((reps, 3)),
            dma((reps, 3)),
            dma((reps, 5)),
            dma((reps, 5)),
            dma((reps - 1,)),
            dma((reps - 1,)),
        ],
        compiler_params=pltpu.CompilerParams(
            collective_id=0, has_side_effects=True, vmem_limit_bytes=62 << 20
        ),
    )(x, sel, gate_up, down.reshape(experts * part, width))[0]


def per_device(hidden_states, routes, gate_prob, gate_up, down):
    groups = lax.axis_size("tok")
    reps = lax.axis_size("rep")
    experts = gate_up.shape[0]
    _, token_count, width = hidden_states.shape
    part = gate_up.shape[2] // 2 // reps
    all_experts = groups * experts
    tokens = hidden_states[0]
    total_bytes = groups * reps * token_count * width * 2
    chunks = max(1, total_bytes // GATHER_BYTES)
    chunk = token_count // chunks

    hit = routes[0][:, :, None] == jnp.arange(all_experts, dtype=jnp.int32)
    weight = jnp.sum(jnp.where(hit, gate_prob[0][:, :, None], 0.0), axis=1)
    sizes = (groups, reps, experts, token_count, width, gate_up.shape[1:], down.shape[1])
    if sizes == (8, 4, 4, 128, 2048, (512, 2048), 256):
        return fused(tokens, weight, gate_up, down, reps)[None]
    gate, up = reshard_gate_up(gate_up, reps)
    stacked_down = down.astype(jnp.bfloat16).reshape(experts * part, width)
    first = lax.axis_index("tok") * experts

    def one_chunk(rows, row_weight):
        everyone = lax.all_gather(rows, ("rep", "tok"), axis=0, tiled=True)
        all_weight = lax.all_gather(row_weight, ("rep", "tok"), axis=0, tiled=True)
        mine = lax.dynamic_slice_in_dim(all_weight, first, experts, 1)
        scale = jnp.repeat(mine, part, axis=1)
        g = jnp.dot(everyone, gate, preferred_element_type=jnp.float32)
        u = jnp.dot(everyone, up, preferred_element_type=jnp.float32)
        units = (jax.nn.silu(g) * u * scale).astype(jnp.bfloat16)
        partial = jnp.dot(units, stacked_down, preferred_element_type=jnp.float32)
        return lax.psum_scatter(
            partial.astype(jnp.bfloat16), ("rep", "tok"), scatter_dimension=0, tiled=True
        )

    if chunks == 1:
        return one_chunk(tokens, weight)[None]
    mixed = lax.map(
        lambda part_of: one_chunk(*part_of),
        (tokens.reshape(chunks, chunk, width), weight.reshape(chunks, chunk, all_experts)),
    )
    return mixed.reshape(1, token_count, width)


def solution(mesh):
    return jax.shard_map(
        per_device,
        mesh=mesh,
        in_specs=(
            P("rep", "tok", None),
            P("rep", "tok", None),
            P("rep", "tok", None),
            P("tok", "rep", None),
            P("tok", "rep", None),
        ),
        out_specs=P("rep", "tok", None),
        check_vma=False,
    )
```

```python
import jax
import jax.numpy as jnp
from jax import lax
from jax.experimental import pallas as pl
from jax.experimental.pallas import tpu as pltpu
from jax.sharding import PartitionSpec as P

GATHER_BYTES = 16 << 20


def reshard_gate_up(gate_up, reps):
    experts, rows, columns = gate_up.shape
    part = columns // 2 // reps
    me = lax.axis_index("rep")
    pieces = (
        gate_up.astype(jnp.bfloat16)
        .reshape(experts, rows, 2, reps, part)
        .transpose(3, 2, 1, 0, 4)
        .reshape(reps, 2, rows, experts * part)
    )
    whole = jnp.zeros((2, reps, rows, experts * part), jnp.bfloat16)
    for shift in range(reps):
        piece = lax.dynamic_index_in_dim(pieces, lax.rem(me + shift, reps), 0, keepdims=False)
        if shift:
            piece = lax.ppermute(piece, "rep", [(i, (i + shift) % reps) for i in range(reps)])
        source = lax.rem(me + reps - shift, reps)
        whole = lax.dynamic_update_slice(whole, piece[:, None], (0, source, 0, 0))
    whole = whole.reshape(2, reps * rows, experts * part)
    return whole[0], whole[1]


LANES = 128
HALVES = 2


def fused_kernel(
    x_ref, sel_ref, gate_ref, down_ref, out_ref, served,
    x, w, d, units, r1, r2, r3, rz, wide, narrow,
    local_sem, load_sem, store_sem, w_send, w_recv, z_send, z_recv, ag_send, ag_recv, rs_send, rs_recv, o_send, o_recv,
):
    reps, _, _, _, rows, _ = x.shape
    experts, depth, both = w.shape
    part = both // 2
    width = d.shape[1]
    block_depth = depth // reps
    ff = gate_ref.shape[2] // 2
    r = lax.axis_index("rep")
    t = lax.axis_index("tok")
    core = lax.rem(t, 2)
    xs = lax.rem(lax.div(t, 2), 2)
    ys = lax.div(t, 4)
    core_mate = {"tok": t + 1 - 2 * core}
    x_mate = {"tok": t + 2 - 4 * xs}
    y_mate = {"tok": t + 4 - 8 * ys}
    rep_mates = [{"rep": lax.rem(r + k, reps)} for k in range(1, reps)]
    across = reps - 1 - r
    beside = r + 1 - 2 * lax.rem(r, 2)
    piece = wide.shape[1]
    other = 1 - core

    barrier = pltpu.get_barrier_semaphore()
    mates = [core_mate, x_mate, y_mate] + rep_mates
    for mate in mates:
        pl.semaphore_signal(barrier, inc=1, device_id=mate, device_id_type=pl.DeviceIdType.MESH)
    pl.semaphore_wait(barrier, len(mates))

    def remote(src, dst, send, recv, mate):
        copy = pltpu.make_async_remote_copy(
            src_ref=src, dst_ref=dst, send_sem=send, recv_sem=recv,
            device_id=mate, device_id_type=pl.DeviceIdType.MESH,
        )
        copy.start()
        return copy

    def local(src, dst, sem):
        copy = pltpu.make_async_copy(src, dst, sem)
        copy.start()
        return copy

    mine = x.at[r, ys, xs, core]
    own_x = local(x_ref, mine, local_sem.at[0])
    from_across = remote(x_ref, mine, z_send.at[0], z_recv.at[0], {"rep": across})
    from_beside = remote(x_ref, mine, z_send.at[1], z_recv.at[1], {"rep": beside})

    def cast_rows(src, dst_store):
        def some(n, carry):
            at = pl.ds(pl.multiple_of(n * 16, 16), 16)
            dst_store(at, n, src[at, :].astype(jnp.bfloat16))
            return carry

        lax.fori_loop(0, piece // 16, some, 0)

    def load(source, n):
        rows_of = pl.ds(n * piece, piece)
        return local(source.at[rows_of, :], wide.at[n % 2], load_sem.at[n % 2])

    def cast_expert(e):
        count = gate_ref.shape[1] // piece
        loads, stores = [load(gate_ref.at[e], 0)], []
        for n in range(count):
            if n + 1 < count:
                loads.append(load(gate_ref.at[e], n + 1))
            loads[n].wait()
            if n >= 2:
                stores[n - 2].wait()

            def keep(at, step, value, slot=n % 2):
                narrow[slot, at, :] = value

            cast_rows(wide.at[n % 2], keep)
            stores.append(
                local(
                    narrow.at[n % 2], served.at[e, pl.ds(n * piece, piece), :], store_sem.at[n % 2]
                )
            )
        for store in stores[-2:]:
            store.wait()

    def cast_down():
        count = d.shape[0] // piece
        loads = [load(down_ref, 0)]
        for n in range(count):
            if n + 1 < count:
                loads.append(load(down_ref, n + 1))
            loads[n].wait()

            def keep(at, step, value, base=n * piece):
                d[pl.ds(pl.multiple_of(base + step * 16, 16), 16), :] = value

            cast_rows(wide.at[n % 2], keep)

    landing = pl.ds(pl.multiple_of(r * block_depth, block_depth), block_depth)

    def send_weights(e):
        copies = []
        for half in range(HALVES):
            into = w.at[e, landing, pl.ds(half * part, part)]
            for k in range(1, reps):
                to = lax.rem(r + k, reps)
                columns = pl.ds(pl.multiple_of(half * ff + to * part, part), part)
                copies.append(
                    remote(
                        served.at[e, :, columns], into,
                        w_send.at[e, k - 1, half], w_recv.at[e, k - 1, half], rep_mates[k - 1],
                    )
                )
            columns = pl.ds(pl.multiple_of(half * ff + r * part, part), part)
            copies.append(
                local(served.at[e, :, columns], into, local_sem.at[2 + HALVES * e + half])
            )
        return copies

    cast_expert(0)
    weights = [send_weights(0)]

    chunk_of = [r, across, beside, reps - 1 - beside]
    stage = []

    def gather_first(i):
        block = x.at[chunk_of[i], ys, xs, core]
        mate = x_mate if i % 2 == 0 else y_mate
        stage.append(remote(block, block, ag_send.at[i, 0], ag_recv.at[i, 0], mate))

    own_x.wait()
    gather_first(0)
    cast_expert(1)
    from_across.wait()
    block = x.at[across, ys, xs, core]
    forwarded = remote(block, block, z_send.at[2], z_recv.at[2], {"rep": beside})
    gather_first(1)
    from_beside.wait()
    gather_first(2)
    weights.append(send_weights(1))
    forwarded.wait()
    gather_first(3)
    cast_expert(2)
    for i in range(reps):
        stage[i].wait()
        if i % 2 == 0:
            block, mate = x.at[chunk_of[i], ys, :, core], y_mate
        else:
            block, mate = x.at[chunk_of[i], :, xs, core], x_mate
        stage[i] = remote(block, block, ag_send.at[i, 1], ag_recv.at[i, 1], mate)

    def arrive(e):
        for copy in weights[e]:
            copy.wait()
        if e + 2 < experts:
            weights.append(send_weights(e + 2))

    arrive(0)
    for i in range(reps):
        stage[i].wait()
        block = x.at[chunk_of[i], :, :, core]
        stage[i] = remote(block, block, ag_send.at[i, 2], ag_recv.at[i, 2], core_mate)
    cast_expert(3)
    cast_down()
    for i in range(reps):
        stage[i].wait()

    def make_units(e, i, half):
        c = lax.rem(r + 1 + i, reps)
        h = other + half * (core - other)
        values = x[c, :, :, h, :, pl.ds(0, width)].reshape(4 * rows, width)
        marks = x[c, :, :, h, :, pl.ds(width, LANES)].reshape(4 * rows, LANES)
        y = jnp.dot(values, w[e], preferred_element_type=jnp.float32)
        scale = jnp.dot(marks, sel_ref[e], preferred_element_type=jnp.float32)
        g, u = y[:, :part], y[:, part:]
        unit = g * (1.0 / (1.0 + jnp.exp(-g))) * u * scale
        units[i, half, :, pl.ds(e * part, part)] = unit.astype(jnp.bfloat16)

    step = 512
    spent = (experts - 1) * part
    ahead = {(0, 0): 0, (0, 1): 1, (1, 0): 2}

    def project_ahead(i, half):
        slot = ahead[i, half]

        def columns_of(n, carry):
            at = pl.ds(pl.multiple_of(n * step, step), step)
            total = jnp.dot(
                units[i, half, :, pl.ds(0, spent)], d[pl.ds(0, spent), at],
                preferred_element_type=jnp.float32,
            )
            w[slot, at, :] = total.astype(jnp.bfloat16)
            return carry

        lax.fori_loop(0, width // step, columns_of, 0)

    def project(i, half, q):
        c = lax.rem(r + 1 + i, reps)
        h = other if half == 0 else core
        slot = ahead.get((i, half))
        below = 0 if slot is None else spent
        depth_of = pl.ds(below, d.shape[0] - below)
        count = width // step // 2

        def columns_of(n, carry):
            columns = pl.ds(pl.multiple_of(n * step, step), step)
            total = jnp.dot(
                units[i, half, :, depth_of], d[depth_of, columns],
                preferred_element_type=jnp.float32,
            )
            if slot is not None:
                total = total + w[slot, columns, :].astype(jnp.float32)
            total = total.reshape(2, 2, rows, step)
            if half:
                total = total + r1[i, :, :, :, columns].astype(jnp.float32)
            x[c, :, :, h, :, columns] = total.astype(jnp.bfloat16)
            return carry

        lax.fori_loop(q * count, (q + 1) * count, columns_of, 0)

    for e in range(experts - 1):
        if e:
            arrive(e)

        def tile(n, carry):
            make_units(e, lax.div(n, 2), lax.rem(n, 2))
            return carry

        lax.fori_loop(0, 2 * reps, tile, 0)
    for i, half in ahead:
        project_ahead(i, half)
    arrive(experts - 1)

    flat = pl.ds(0, width)
    streams = [pl.ds(q * (width // 2), width // 2) for q in range(2)]
    first, second, third, last = {}, {}, {}, []

    def scatter_core(i):
        make_units(experts - 1, i, 0)
        c = lax.rem(r + 1 + i, reps)
        for q, columns in enumerate(streams):
            project(i, 0, q)
            first[i, q] = remote(
                x.at[c, :, :, other, :, columns], r1.at[i, :, :, :, columns],
                rs_send.at[i, q], rs_recv.at[i, q], core_mate,
            )

    def scatter_second(i):
        make_units(experts - 1, i, 1)
        c = lax.rem(r + 1 + i, reps)
        for q, columns in enumerate(streams):
            first[i, q].wait_recv()
            project(i, 1, q)
            if q == 0:
                src, mate = x.at[c, :, 1 - xs, core, :, columns], x_mate
            else:
                src, mate = x.at[c, 1 - ys, :, core, :, columns], y_mate
            second[i, q] = remote(
                src, r2.at[i, :, :, columns], rs_send.at[i, 2 + q], rs_recv.at[i, 2 + q], mate
            )

    def scatter_third(i):
        c = lax.rem(r + 1 + i, reps)
        for q, columns in enumerate(streams):
            second[i, q].wait_recv()

            def add(n, carry, q=q, columns=columns):
                at = pl.ds(pl.multiple_of(n * 16, 16), 16)
                for k in range(2):
                    where = (c, k, xs, core, at, columns) if q == 0 else (c, ys, k, core, at, columns)
                    total = x[where].astype(jnp.float32) + r2[i, k, at, columns].astype(jnp.float32)
                    x[where] = total.astype(jnp.bfloat16)
                return carry

            lax.fori_loop(0, rows // 16, add, 0)
            if q == 0:
                src, mate = x.at[c, 1 - ys, xs, core, :, columns], y_mate
            else:
                src, mate = x.at[c, ys, 1 - xs, core, :, columns], x_mate
            third[i, q] = remote(
                src, r3.at[i, :, columns], rs_send.at[i, 4 + q], rs_recv.at[i, 4 + q], mate
            )

    def scatter_rep(i):
        for q in range(2):
            third[i, q].wait_recv()
        c = lax.rem(r + 1 + i, reps)
        if i == reps - 1:
            return

        def add(n, carry):
            at = pl.ds(pl.multiple_of(n * 16, 16), 16)
            where = (c, ys, xs, core, at, flat)
            total = x[where].astype(jnp.float32) + r3[i, at, :].astype(jnp.float32)
            x[where] = total.astype(jnp.bfloat16)
            return carry

        lax.fori_loop(0, rows // 16, add, 0)
        last.append(
            remote(
                x.at[c, ys, xs, core, :, flat], rz.at[i], o_send.at[i], o_recv.at[i], rep_mates[i]
            )
        )

    order = [
        (scatter_core, 0), (scatter_second, 0), (scatter_core, 1), (scatter_core, 2),
        (scatter_second, 1), (scatter_core, 3), (scatter_second, 2), (scatter_third, 0),
        (scatter_second, 3), (scatter_third, 1), (scatter_rep, 0), (scatter_third, 2),
        (scatter_rep, 1), (scatter_third, 3), (scatter_rep, 2), (scatter_rep, 3),
    ]
    for work, i in order:
        work(i)
    for copy in last:
        copy.wait_recv()

    def finish(n, carry):
        at = pl.ds(pl.multiple_of(n * 16, 16), 16)
        total = x[r, ys, xs, core, at, flat].astype(jnp.float32)
        total = total + r3[reps - 1, at, :].astype(jnp.float32)
        for k in range(reps - 1):
            total = total + rz[k, at, :].astype(jnp.float32)
        out_ref[at, :] = total.astype(jnp.bfloat16)
        return carry

    lax.fori_loop(0, rows // 16, finish, 0)
    for copy in list(first.values()) + list(second.values()) + list(third.values()) + last:
        copy.wait_send()


def fused(tokens, weight, gate_up, down, reps):
    rows, width = tokens.shape
    experts, block_depth, columns = gate_up.shape
    part = columns // 2 // reps
    all_experts = weight.shape[1]
    high = lax.reduce_precision(weight, 8, 7)
    marks = jnp.concatenate([high, weight - high], axis=1).astype(jnp.bfloat16)
    marks = jnp.pad(marks, ((0, 0), (0, LANES - 2 * all_experts)))
    x = jnp.concatenate([tokens, marks], axis=1)
    lane = jnp.arange(LANES, dtype=jnp.int32)
    own = lax.axis_index("tok") * experts + jnp.arange(experts, dtype=jnp.int32)
    chosen = (lane[None, :] == own[:, None]) | (lane[None, :] == own[:, None] + all_experts)
    sel = jnp.broadcast_to(chosen[:, :, None], (experts, LANES, part)).astype(jnp.bfloat16)
    depth = block_depth * reps
    bf16 = jnp.bfloat16
    dma = pltpu.SemaphoreType.DMA
    hbm = pl.BlockSpec(memory_space=pl.ANY)
    vmem = pl.BlockSpec(memory_space=pltpu.VMEM)
    return pl.pallas_call(
        fused_kernel,
        out_shape=[
            jax.ShapeDtypeStruct((rows, width), bf16),
            jax.ShapeDtypeStruct(gate_up.shape, bf16),
        ],
        in_specs=[hbm, vmem, hbm, hbm],
        out_specs=[vmem, hbm],
        scratch_shapes=[
            pltpu.VMEM((reps, 2, 2, 2, rows, width + LANES), bf16),
            pltpu.VMEM((experts, depth, 2 * part), bf16),
            pltpu.VMEM((experts * part, width), bf16),
            pltpu.VMEM((reps, 2, 4 * rows, experts * part), bf16),
            pltpu.VMEM((reps, 2, 2, rows, width), bf16),
            pltpu.VMEM((reps, 2, rows, width), bf16),
            pltpu.VMEM((reps, rows, width), bf16),
            pltpu.VMEM((reps - 1, rows, width), bf16),
            pltpu.VMEM((2, 128, columns), jnp.float32),
            pltpu.VMEM((2, 128, columns), bf16),
            dma((2 + HALVES * experts,)),
            dma((2,)),
            dma((2,)),
            dma((experts, reps - 1, HALVES)),
            dma((experts, reps - 1, HALVES)),
            dma((reps - 1,)),
            dma((reps - 1,)),
            dma((reps, 3)),
            dma((reps, 3)),
            dma((reps, 6)),
            dma((reps, 6)),
            dma((reps - 1,)),
            dma((reps - 1,)),
        ],
        compiler_params=pltpu.CompilerParams(
            collective_id=0, has_side_effects=True, vmem_limit_bytes=62 << 20
        ),
    )(x, sel, gate_up, down.reshape(experts * part, width))[0]


def per_device(hidden_states, routes, gate_prob, gate_up, down):
    groups = lax.axis_size("tok")
    reps = lax.axis_size("rep")
    experts = gate_up.shape[0]
    _, token_count, width = hidden_states.shape
    part = gate_up.shape[2] // 2 // reps
    all_experts = groups * experts
    tokens = hidden_states[0]
    total_bytes = groups * reps * token_count * width * 2
    chunks = max(1, total_bytes // GATHER_BYTES)
    chunk = token_count // chunks

    hit = routes[0][:, :, None] == jnp.arange(all_experts, dtype=jnp.int32)
    weight = jnp.sum(jnp.where(hit, gate_prob[0][:, :, None], 0.0), axis=1)
    sizes = (groups, reps, experts, token_count, width, gate_up.shape[1:], down.shape[1])
    if sizes == (8, 4, 4, 128, 2048, (512, 2048), 256):
        return fused(tokens, weight, gate_up, down, reps)[None]
    gate, up = reshard_gate_up(gate_up, reps)
    stacked_down = down.astype(jnp.bfloat16).reshape(experts * part, width)
    first = lax.axis_index("tok") * experts

    def one_chunk(rows, row_weight):
        everyone = lax.all_gather(rows, ("rep", "tok"), axis=0, tiled=True)
        all_weight = lax.all_gather(row_weight, ("rep", "tok"), axis=0, tiled=True)
        mine = lax.dynamic_slice_in_dim(all_weight, first, experts, 1)
        scale = jnp.repeat(mine, part, axis=1)
        g = jnp.dot(everyone, gate, preferred_element_type=jnp.float32)
        u = jnp.dot(everyone, up, preferred_element_type=jnp.float32)
        units = (jax.nn.silu(g) * u * scale).astype(jnp.bfloat16)
        partial = jnp.dot(units, stacked_down, preferred_element_type=jnp.float32)
        return lax.psum_scatter(
            partial.astype(jnp.bfloat16), ("rep", "tok"), scatter_dimension=0, tiled=True
        )

    if chunks == 1:
        return one_chunk(tokens, weight)[None]
    mixed = lax.map(
        lambda part_of: one_chunk(*part_of),
        (tokens.reshape(chunks, chunk, width), weight.reshape(chunks, chunk, all_experts)),
    )
    return mixed.reshape(1, token_count, width)


def solution(mesh):
    return jax.shard_map(
        per_device,
        mesh=mesh,
        in_specs=(
            P("rep", "tok", None),
            P("rep", "tok", None),
            P("rep", "tok", None),
            P("tok", "rep", None),
            P("tok", "rep", None),
        ),
        out_specs=P("rep", "tok", None),
        check_vma=False,
    )
```

```python
import jax
import jax.numpy as jnp
from jax import lax
from jax.experimental import pallas as pl
from jax.experimental.pallas import tpu as pltpu
from jax.sharding import PartitionSpec as P

GATHER_BYTES = 16 << 20


def reshard_gate_up(gate_up, reps):
    experts, rows, columns = gate_up.shape
    part = columns // 2 // reps
    me = lax.axis_index("rep")
    pieces = (
        gate_up.astype(jnp.bfloat16)
        .reshape(experts, rows, 2, reps, part)
        .transpose(3, 2, 1, 0, 4)
        .reshape(reps, 2, rows, experts * part)
    )
    whole = jnp.zeros((2, reps, rows, experts * part), jnp.bfloat16)
    for shift in range(reps):
        piece = lax.dynamic_index_in_dim(pieces, lax.rem(me + shift, reps), 0, keepdims=False)
        if shift:
            piece = lax.ppermute(piece, "rep", [(i, (i + shift) % reps) for i in range(reps)])
        source = lax.rem(me + reps - shift, reps)
        whole = lax.dynamic_update_slice(whole, piece[:, None], (0, source, 0, 0))
    whole = whole.reshape(2, reps * rows, experts * part)
    return whole[0], whole[1]


LANES = 128
HALVES = 2


def fused_kernel(
    x_ref, sel_ref, gate_ref, down_ref, out_ref, served,
    x, w, d, units, r1, r2, r3, rz, wide, narrow,
    local_sem, load_sem, store_sem, w_send, w_recv, z_send, z_recv, ag_send, ag_recv, rs_send, rs_recv, o_send, o_recv,
):
    reps, _, _, _, rows, _ = x.shape
    experts, depth, both = w.shape
    part = both // 2
    width = d.shape[1]
    block_depth = depth // reps
    ff = gate_ref.shape[2] // 2
    r = lax.axis_index("rep")
    t = lax.axis_index("tok")
    core = lax.rem(t, 2)
    xs = lax.rem(lax.div(t, 2), 2)
    ys = lax.div(t, 4)
    core_mate = {"tok": t + 1 - 2 * core}
    x_mate = {"tok": t + 2 - 4 * xs}
    y_mate = {"tok": t + 4 - 8 * ys}
    rep_mates = [{"rep": lax.rem(r + k, reps)} for k in range(1, reps)]
    across = reps - 1 - r
    beside = r + 1 - 2 * lax.rem(r, 2)
    piece = wide.shape[1]
    other = 1 - core

    barrier = pltpu.get_barrier_semaphore()
    mates = [core_mate, x_mate, y_mate] + rep_mates
    for mate in mates:
        pl.semaphore_signal(barrier, inc=1, device_id=mate, device_id_type=pl.DeviceIdType.MESH)
    pl.semaphore_wait(barrier, len(mates))

    def remote(src, dst, send, recv, mate):
        copy = pltpu.make_async_remote_copy(
            src_ref=src, dst_ref=dst, send_sem=send, recv_sem=recv,
            device_id=mate, device_id_type=pl.DeviceIdType.MESH,
        )
        copy.start()
        return copy

    def local(src, dst, sem):
        copy = pltpu.make_async_copy(src, dst, sem)
        copy.start()
        return copy

    mine = x.at[r, ys, xs, core]
    own_x = local(x_ref, mine, local_sem.at[0])
    from_across = remote(x_ref, mine, z_send.at[0], z_recv.at[0], {"rep": across})
    from_beside = remote(x_ref, mine, z_send.at[1], z_recv.at[1], {"rep": beside})

    def cast_rows(src, dst_store):
        def some(n, carry):
            at = pl.ds(pl.multiple_of(n * 16, 16), 16)
            dst_store(at, n, src[at, :].astype(jnp.bfloat16))
            return carry

        lax.fori_loop(0, piece // 16, some, 0)

    def load(source, n):
        rows_of = pl.ds(n * piece, piece)
        return local(source.at[rows_of, :], wide.at[n % 2], load_sem.at[n % 2])

    def cast_expert(e):
        count = gate_ref.shape[1] // piece
        loads, stores = [load(gate_ref.at[e], 0)], []
        for n in range(count):
            if n + 1 < count:
                loads.append(load(gate_ref.at[e], n + 1))
            loads[n].wait()
            if n >= 2:
                stores[n - 2].wait()

            def keep(at, step, value, slot=n % 2):
                narrow[slot, at, :] = value

            cast_rows(wide.at[n % 2], keep)
            stores.append(
                local(
                    narrow.at[n % 2], served.at[e, pl.ds(n * piece, piece), :], store_sem.at[n % 2]
                )
            )
        for store in stores[-2:]:
            store.wait()

    def cast_down():
        count = d.shape[0] // piece
        loads = [load(down_ref, 0)]
        for n in range(count):
            if n + 1 < count:
                loads.append(load(down_ref, n + 1))
            loads[n].wait()

            def keep(at, step, value, base=n * piece):
                d[pl.ds(pl.multiple_of(base + step * 16, 16), 16), :] = value

            cast_rows(wide.at[n % 2], keep)

    landing = pl.ds(pl.multiple_of(r * block_depth, block_depth), block_depth)

    def send_weights(e):
        copies = []
        for half in range(HALVES):
            into = w.at[e, landing, pl.ds(half * part, part)]
            for k in range(1, reps):
                to = lax.rem(r + k, reps)
                columns = pl.ds(pl.multiple_of(half * ff + to * part, part), part)
                copies.append(
                    remote(
                        served.at[e, :, columns], into,
                        w_send.at[e, k - 1, half], w_recv.at[e, k - 1, half], rep_mates[k - 1],
                    )
                )
            columns = pl.ds(pl.multiple_of(half * ff + r * part, part), part)
            copies.append(
                local(served.at[e, :, columns], into, local_sem.at[2 + HALVES * e + half])
            )
        return copies

    cast_expert(0)

    chunk_of = [r, across, beside, reps - 1 - beside]
    stage = [None] * reps
    weights = []

    def gather_first(i):
        block = x.at[chunk_of[i], ys, xs, core]
        mate = x_mate if i % 2 == 0 else y_mate
        stage[i] = remote(block, block, ag_send.at[i, 0], ag_recv.at[i, 0], mate)

    def gather_second(i):
        stage[i].wait()
        if i % 2 == 0:
            block, mate = x.at[chunk_of[i], ys, :, core], y_mate
        else:
            block, mate = x.at[chunk_of[i], :, xs, core], x_mate
        stage[i] = remote(block, block, ag_send.at[i, 1], ag_recv.at[i, 1], mate)

    def gather_core(i):
        stage[i].wait()
        block = x.at[chunk_of[i], :, :, core]
        stage[i] = remote(block, block, ag_send.at[i, 2], ag_recv.at[i, 2], core_mate)

    def arrive(e):
        for copy in weights[e]:
            copy.wait()
        if e + 2 < experts:
            weights.append(send_weights(e + 2))

    own_x.wait()
    gather_first(0)
    cast_expert(1)
    from_across.wait()
    block = x.at[across, ys, xs, core]
    forwarded = remote(block, block, z_send.at[2], z_recv.at[2], {"rep": beside})
    weights.append(send_weights(0))
    gather_first(1)
    from_beside.wait()
    gather_first(2)
    for i in range(reps - 1):
        gather_second(i)
    weights.append(send_weights(1))
    cast_expert(2)
    forwarded.wait()
    gather_first(3)
    for i in range(reps - 1):
        gather_core(i)
    arrive(0)
    gather_second(3)
    cast_expert(3)
    gather_core(3)
    cast_down()

    def make_units(e, i, half):
        c = lax.rem(r + 1 + i, reps)
        h = other + half * (core - other)
        values = x[c, :, :, h, :, pl.ds(0, width)].reshape(4 * rows, width)
        marks = x[c, :, :, h, :, pl.ds(width, LANES)].reshape(4 * rows, LANES)
        y = jnp.dot(values, w[e], preferred_element_type=jnp.float32)
        scale = jnp.dot(marks, sel_ref[e], preferred_element_type=jnp.float32)
        g, u = y[:, :part], y[:, part:]
        unit = g * (1.0 / (1.0 + jnp.exp(-g))) * u * scale
        units[i, half, :, pl.ds(e * part, part)] = unit.astype(jnp.bfloat16)

    step = 512
    spent = (experts - 1) * part
    ahead = {(0, 0): 0, (1, 0): 1, (2, 0): 2}

    def project_ahead(i, half):
        slot = ahead[i, half]

        def columns_of(n, carry):
            at = pl.ds(pl.multiple_of(n * step, step), step)
            total = jnp.dot(
                units[i, half, :, pl.ds(0, spent)], d[pl.ds(0, spent), at],
                preferred_element_type=jnp.float32,
            )
            w[slot, at, :] = total.astype(jnp.bfloat16)
            return carry

        lax.fori_loop(0, width // step, columns_of, 0)

    def project(i, half, q):
        c = lax.rem(r + 1 + i, reps)
        h = other if half == 0 else core
        slot = ahead.get((i, half))
        below = 0 if slot is None else spent
        depth_of = pl.ds(below, d.shape[0] - below)
        count = width // step // 2

        def columns_of(n, carry):
            columns = pl.ds(pl.multiple_of(n * step, step), step)
            total = jnp.dot(
                units[i, half, :, depth_of], d[depth_of, columns],
                preferred_element_type=jnp.float32,
            )
            if slot is not None:
                total = total + w[slot, columns, :].astype(jnp.float32)
            total = total.reshape(2, 2, rows, step)
            if half:
                total = total + r1[i, :, :, :, columns].astype(jnp.float32)
            x[c, :, :, h, :, columns] = total.astype(jnp.bfloat16)
            return carry

        lax.fori_loop(q * count, (q + 1) * count, columns_of, 0)

    for i in range(reps):
        stage[i].wait()
        place = lax.rem(chunk_of[i] + 2 * reps - r - 1, reps)

        def half_tile(half, carry, place=place):
            make_units(0, place, half)
            return carry

        lax.fori_loop(0, 2, half_tile, 0)
    for e in range(1, experts - 1):
        arrive(e)

        def tile(n, carry, e=e):
            make_units(e, lax.div(n, 2), lax.rem(n, 2))
            return carry

        lax.fori_loop(0, 2 * reps, tile, 0)
    for i, half in ahead:
        project_ahead(i, half)
    arrive(experts - 1)

    flat = pl.ds(0, width)
    streams = [pl.ds(q * (width // 2), width // 2) for q in range(2)]
    first, second, third, last = {}, {}, {}, []

    def scatter_core(i):
        make_units(experts - 1, i, 0)
        c = lax.rem(r + 1 + i, reps)
        for q, columns in enumerate(streams):
            project(i, 0, q)
            first[i, q] = remote(
                x.at[c, :, :, other, :, columns], r1.at[i, :, :, :, columns],
                rs_send.at[i, q], rs_recv.at[i, q], core_mate,
            )

    def scatter_second(i):
        make_units(experts - 1, i, 1)
        c = lax.rem(r + 1 + i, reps)
        for q, columns in enumerate(streams):
            first[i, q].wait_recv()
            project(i, 1, q)
            if q == 0:
                src, mate = x.at[c, :, 1 - xs, core, :, columns], x_mate
            else:
                src, mate = x.at[c, 1 - ys, :, core, :, columns], y_mate
            second[i, q] = remote(
                src, r2.at[i, :, :, columns], rs_send.at[i, 2 + q], rs_recv.at[i, 2 + q], mate
            )

    def scatter_third(i):
        c = lax.rem(r + 1 + i, reps)
        for q, columns in enumerate(streams):
            second[i, q].wait_recv()

            def add(n, carry, q=q, columns=columns):
                at = pl.ds(pl.multiple_of(n * 16, 16), 16)
                for k in range(2):
                    where = (c, k, xs, core, at, columns) if q == 0 else (c, ys, k, core, at, columns)
                    total = x[where].astype(jnp.float32) + r2[i, k, at, columns].astype(jnp.float32)
                    x[where] = total.astype(jnp.bfloat16)
                return carry

            lax.fori_loop(0, rows // 16, add, 0)
            if q == 0:
                src, mate = x.at[c, 1 - ys, xs, core, :, columns], y_mate
            else:
                src, mate = x.at[c, ys, 1 - xs, core, :, columns], x_mate
            third[i, q] = remote(
                src, r3.at[i, :, columns], rs_send.at[i, 4 + q], rs_recv.at[i, 4 + q], mate
            )

    def scatter_rep(i):
        for q in range(2):
            third[i, q].wait_recv()
        c = lax.rem(r + 1 + i, reps)
        if i == reps - 1:
            return

        def add(n, carry):
            at = pl.ds(pl.multiple_of(n * 16, 16), 16)
            where = (c, ys, xs, core, at, flat)
            total = x[where].astype(jnp.float32) + r3[i, at, :].astype(jnp.float32)
            x[where] = total.astype(jnp.bfloat16)
            return carry

        lax.fori_loop(0, rows // 16, add, 0)
        last.append(
            remote(
                x.at[c, ys, xs, core, :, flat], rz.at[i], o_send.at[i], o_recv.at[i], rep_mates[i]
            )
        )

    order = [
        (scatter_core, 0), (scatter_core, 1), (scatter_core, 2), (scatter_second, 0),
        (scatter_core, 3), (scatter_second, 1), (scatter_second, 2), (scatter_third, 0),
        (scatter_second, 3), (scatter_third, 1), (scatter_rep, 0), (scatter_third, 2),
        (scatter_rep, 1), (scatter_third, 3), (scatter_rep, 2), (scatter_rep, 3),
    ]
    for work, i in order:
        work(i)
    for copy in last:
        copy.wait_recv()

    def finish(n, carry):
        at = pl.ds(pl.multiple_of(n * 16, 16), 16)
        total = x[r, ys, xs, core, at, flat].astype(jnp.float32)
        total = total + r3[reps - 1, at, :].astype(jnp.float32)
        for k in range(reps - 1):
            total = total + rz[k, at, :].astype(jnp.float32)
        out_ref[at, :] = total.astype(jnp.bfloat16)
        return carry

    lax.fori_loop(0, rows // 16, finish, 0)
    for copy in list(first.values()) + list(second.values()) + list(third.values()) + last:
        copy.wait_send()


def fused(tokens, weight, gate_up, down, reps):
    rows, width = tokens.shape
    experts, block_depth, columns = gate_up.shape
    part = columns // 2 // reps
    all_experts = weight.shape[1]
    high = lax.reduce_precision(weight, 8, 7)
    marks = jnp.concatenate([high, weight - high], axis=1).astype(jnp.bfloat16)
    marks = jnp.pad(marks, ((0, 0), (0, LANES - 2 * all_experts)))
    x = jnp.concatenate([tokens, marks], axis=1)
    lane = jnp.arange(LANES, dtype=jnp.int32)
    own = lax.axis_index("tok") * experts + jnp.arange(experts, dtype=jnp.int32)
    chosen = (lane[None, :] == own[:, None]) | (lane[None, :] == own[:, None] + all_experts)
    sel = jnp.broadcast_to(chosen[:, :, None], (experts, LANES, part)).astype(jnp.bfloat16)
    depth = block_depth * reps
    bf16 = jnp.bfloat16
    dma = pltpu.SemaphoreType.DMA
    hbm = pl.BlockSpec(memory_space=pl.ANY)
    vmem = pl.BlockSpec(memory_space=pltpu.VMEM)
    return pl.pallas_call(
        fused_kernel,
        out_shape=[
            jax.ShapeDtypeStruct((rows, width), bf16),
            jax.ShapeDtypeStruct(gate_up.shape, bf16),
        ],
        in_specs=[hbm, vmem, hbm, hbm],
        out_specs=[vmem, hbm],
        scratch_shapes=[
            pltpu.VMEM((reps, 2, 2, 2, rows, width + LANES), bf16),
            pltpu.VMEM((experts, depth, 2 * part), bf16),
            pltpu.VMEM((experts * part, width), bf16),
            pltpu.VMEM((reps, 2, 4 * rows, experts * part), bf16),
            pltpu.VMEM((reps, 2, 2, rows, width), bf16),
            pltpu.VMEM((reps, 2, rows, width), bf16),
            pltpu.VMEM((reps, rows, width), bf16),
            pltpu.VMEM((reps - 1, rows, width), bf16),
            pltpu.VMEM((2, 128, columns), jnp.float32),
            pltpu.VMEM((2, 128, columns), bf16),
            dma((2 + HALVES * experts,)),
            dma((2,)),
            dma((2,)),
            dma((experts, reps - 1, HALVES)),
            dma((experts, reps - 1, HALVES)),
            dma((reps - 1,)),
            dma((reps - 1,)),
            dma((reps, 3)),
            dma((reps, 3)),
            dma((reps, 6)),
            dma((reps, 6)),
            dma((reps - 1,)),
            dma((reps - 1,)),
        ],
        compiler_params=pltpu.CompilerParams(
            collective_id=0, has_side_effects=True, vmem_limit_bytes=62 << 20
        ),
    )(x, sel, gate_up, down.reshape(experts * part, width))[0]


def per_device(hidden_states, routes, gate_prob, gate_up, down):
    groups = lax.axis_size("tok")
    reps = lax.axis_size("rep")
    experts = gate_up.shape[0]
    _, token_count, width = hidden_states.shape
    part = gate_up.shape[2] // 2 // reps
    all_experts = groups * experts
    tokens = hidden_states[0]
    total_bytes = groups * reps * token_count * width * 2
    chunks = max(1, total_bytes // GATHER_BYTES)
    chunk = token_count // chunks

    hit = routes[0][:, :, None] == jnp.arange(all_experts, dtype=jnp.int32)
    weight = jnp.sum(jnp.where(hit, gate_prob[0][:, :, None], 0.0), axis=1)
    sizes = (groups, reps, experts, token_count, width, gate_up.shape[1:], down.shape[1])
    if sizes == (8, 4, 4, 128, 2048, (512, 2048), 256):
        return fused(tokens, weight, gate_up, down, reps)[None]
    gate, up = reshard_gate_up(gate_up, reps)
    stacked_down = down.astype(jnp.bfloat16).reshape(experts * part, width)
    first = lax.axis_index("tok") * experts

    def one_chunk(rows, row_weight):
        everyone = lax.all_gather(rows, ("rep", "tok"), axis=0, tiled=True)
        all_weight = lax.all_gather(row_weight, ("rep", "tok"), axis=0, tiled=True)
        mine = lax.dynamic_slice_in_dim(all_weight, first, experts, 1)
        scale = jnp.repeat(mine, part, axis=1)
        g = jnp.dot(everyone, gate, preferred_element_type=jnp.float32)
        u = jnp.dot(everyone, up, preferred_element_type=jnp.float32)
        units = (jax.nn.silu(g) * u * scale).astype(jnp.bfloat16)
        partial = jnp.dot(units, stacked_down, preferred_element_type=jnp.float32)
        return lax.psum_scatter(
            partial.astype(jnp.bfloat16), ("rep", "tok"), scatter_dimension=0, tiled=True
        )

    if chunks == 1:
        return one_chunk(tokens, weight)[None]
    mixed = lax.map(
        lambda part_of: one_chunk(*part_of),
        (tokens.reshape(chunks, chunk, width), weight.reshape(chunks, chunk, all_experts)),
    )
    return mixed.reshape(1, token_count, width)


def solution(mesh):
    return jax.shard_map(
        per_device,
        mesh=mesh,
        in_specs=(
            P("rep", "tok", None),
            P("rep", "tok", None),
            P("rep", "tok", None),
            P("tok", "rep", None),
            P("tok", "rep", None),
        ),
        out_specs=P("rep", "tok", None),
        check_vma=False,
    )
```

```python
import jax
import jax.numpy as jnp
from jax import lax
from jax.experimental import pallas as pl
from jax.experimental.pallas import tpu as pltpu
from jax.sharding import PartitionSpec as P

GATHER_BYTES = 16 << 20


def reshard_gate_up(gate_up, reps):
    experts, rows, columns = gate_up.shape
    part = columns // 2 // reps
    me = lax.axis_index("rep")
    pieces = (
        gate_up.astype(jnp.bfloat16)
        .reshape(experts, rows, 2, reps, part)
        .transpose(3, 2, 1, 0, 4)
        .reshape(reps, 2, rows, experts * part)
    )
    whole = jnp.zeros((2, reps, rows, experts * part), jnp.bfloat16)
    for shift in range(reps):
        piece = lax.dynamic_index_in_dim(pieces, lax.rem(me + shift, reps), 0, keepdims=False)
        if shift:
            piece = lax.ppermute(piece, "rep", [(i, (i + shift) % reps) for i in range(reps)])
        source = lax.rem(me + reps - shift, reps)
        whole = lax.dynamic_update_slice(whole, piece[:, None], (0, source, 0, 0))
    whole = whole.reshape(2, reps * rows, experts * part)
    return whole[0], whole[1]


LANES = 128
HALVES = 2


def fused_kernel(
    x_ref, sel_ref, gate_ref, down_ref, out_ref, served,
    x, w, d, units, r1, r2, r3, rz, wide, narrow,
    local_sem, load_sem, store_sem, w_send, w_recv, z_send, z_recv, ag_send, ag_recv, rs_send, rs_recv, o_send, o_recv,
):
    reps, _, _, _, rows, _ = x.shape
    experts, depth, both = w.shape
    part = both // 2
    width = d.shape[1]
    block_depth = depth // reps
    ff = gate_ref.shape[2] // 2
    r = lax.axis_index("rep")
    t = lax.axis_index("tok")
    core = lax.rem(t, 2)
    xs = lax.rem(lax.div(t, 2), 2)
    ys = lax.div(t, 4)
    core_mate = {"tok": t + 1 - 2 * core}
    x_mate = {"tok": t + 2 - 4 * xs}
    y_mate = {"tok": t + 4 - 8 * ys}
    rep_mates = [{"rep": lax.rem(r + k, reps)} for k in range(1, reps)]
    across = reps - 1 - r
    beside = r + 1 - 2 * lax.rem(r, 2)
    piece = wide.shape[1]
    other = 1 - core

    barrier = pltpu.get_barrier_semaphore()
    mates = [core_mate, x_mate, y_mate] + rep_mates
    for mate in mates:
        pl.semaphore_signal(barrier, inc=1, device_id=mate, device_id_type=pl.DeviceIdType.MESH)
    pl.semaphore_wait(barrier, len(mates))

    def remote(src, dst, send, recv, mate):
        copy = pltpu.make_async_remote_copy(
            src_ref=src, dst_ref=dst, send_sem=send, recv_sem=recv,
            device_id=mate, device_id_type=pl.DeviceIdType.MESH,
        )
        copy.start()
        return copy

    def local(src, dst, sem):
        copy = pltpu.make_async_copy(src, dst, sem)
        copy.start()
        return copy

    mine = x.at[r, ys, xs, core]
    own_x = local(x_ref, mine, local_sem.at[0])
    from_across = remote(x_ref, mine, z_send.at[0], z_recv.at[0], {"rep": across})
    from_beside = remote(x_ref, mine, z_send.at[1], z_recv.at[1], {"rep": beside})

    def cast_rows(src, dst_store):
        def some(n, carry):
            at = pl.ds(pl.multiple_of(n * 16, 16), 16)
            dst_store(at, n, src[at, :].astype(jnp.bfloat16))
            return carry

        lax.fori_loop(0, piece // 16, some, 0)

    def load(source, n):
        rows_of = pl.ds(n * piece, piece)
        return local(source.at[rows_of, :], wide.at[n % 2], load_sem.at[n % 2])

    def cast_expert(e):
        count = gate_ref.shape[1] // piece
        loads, stores = [load(gate_ref.at[e], 0)], []
        for n in range(count):
            if n + 1 < count:
                loads.append(load(gate_ref.at[e], n + 1))
            loads[n].wait()
            if n >= 2:
                stores[n - 2].wait()

            def keep(at, step, value, slot=n % 2):
                narrow[slot, at, :] = value

            cast_rows(wide.at[n % 2], keep)
            stores.append(
                local(
                    narrow.at[n % 2], served.at[e, pl.ds(n * piece, piece), :], store_sem.at[n % 2]
                )
            )
        for store in stores[-2:]:
            store.wait()

    def cast_down():
        count = d.shape[0] // piece
        loads = [load(down_ref, 0)]
        for n in range(count):
            if n + 1 < count:
                loads.append(load(down_ref, n + 1))
            loads[n].wait()

            def keep(at, step, value, base=n * piece):
                d[pl.ds(pl.multiple_of(base + step * 16, 16), 16), :] = value

            cast_rows(wide.at[n % 2], keep)

    landing = pl.ds(pl.multiple_of(r * block_depth, block_depth), block_depth)

    def send_weights(e):
        copies = []
        for half in range(HALVES):
            into = w.at[e, landing, pl.ds(half * part, part)]
            for k in range(1, reps):
                to = lax.rem(r + k, reps)
                columns = pl.ds(pl.multiple_of(half * ff + to * part, part), part)
                copies.append(
                    remote(
                        served.at[e, :, columns], into,
                        w_send.at[e, k - 1, half], w_recv.at[e, k - 1, half], rep_mates[k - 1],
                    )
                )
            columns = pl.ds(pl.multiple_of(half * ff + r * part, part), part)
            copies.append(
                local(served.at[e, :, columns], into, local_sem.at[2 + HALVES * e + half])
            )
        return copies

    cast_expert(0)
    weights = [send_weights(0)]

    chunk_of = [r, across, beside, reps - 1 - beside]
    stage = []

    def gather_first(i):
        block = x.at[chunk_of[i], ys, xs, core]
        mate = x_mate if i % 2 == 0 else y_mate
        stage.append(remote(block, block, ag_send.at[i, 0], ag_recv.at[i, 0], mate))

    own_x.wait()
    gather_first(0)
    cast_expert(1)
    weights.append(send_weights(1))
    from_across.wait()
    block = x.at[across, ys, xs, core]
    forwarded = remote(block, block, z_send.at[2], z_recv.at[2], {"rep": beside})
    gather_first(1)
    from_beside.wait()
    gather_first(2)
    forwarded.wait()
    gather_first(3)
    cast_expert(2)
    for i in range(reps):
        stage[i].wait()
        if i % 2 == 0:
            block, mate = x.at[chunk_of[i], ys, :, core], y_mate
        else:
            block, mate = x.at[chunk_of[i], :, xs, core], x_mate
        stage[i] = remote(block, block, ag_send.at[i, 1], ag_recv.at[i, 1], mate)

    def arrive(e):
        for copy in weights[e]:
            copy.wait()
        if e + 2 < experts:
            weights.append(send_weights(e + 2))

    arrive(0)
    for i in range(reps):
        stage[i].wait()
        block = x.at[chunk_of[i], :, :, core]
        stage[i] = remote(block, block, ag_send.at[i, 2], ag_recv.at[i, 2], core_mate)
    cast_expert(3)
    cast_down()
    for i in range(reps):
        stage[i].wait()

    def make_units(e, i, half):
        c = lax.rem(r + 1 + i, reps)
        h = other + half * (core - other)
        values = x[c, :, :, h, :, pl.ds(0, width)].reshape(4 * rows, width)
        marks = x[c, :, :, h, :, pl.ds(width, LANES)].reshape(4 * rows, LANES)
        y = jnp.dot(values, w[e], preferred_element_type=jnp.float32)
        scale = jnp.dot(marks, sel_ref[e], preferred_element_type=jnp.float32)
        g, u = y[:, :part], y[:, part:]
        unit = g * (1.0 / (1.0 + jnp.exp(-g))) * u * scale
        units[i, half, :, pl.ds(e * part, part)] = unit.astype(jnp.bfloat16)

    def project(i, half):
        c = lax.rem(r + 1 + i, reps)
        h = other if half == 0 else core
        step = 512

        def columns_of(n, carry):
            columns = pl.ds(pl.multiple_of(n * step, step), step)
            total = jnp.dot(units[i, half], d[:, columns], preferred_element_type=jnp.float32)
            total = total.reshape(2, 2, rows, step)
            if half:
                total = total + r1[i, :, :, :, columns].astype(jnp.float32)
            x[c, :, :, h, :, columns] = total.astype(jnp.bfloat16)
            return carry

        lax.fori_loop(0, width // step, columns_of, 0)

    for e in range(experts - 1):
        if e:
            arrive(e)

        def tile(n, carry):
            make_units(e, lax.div(n, 2), lax.rem(n, 2))
            return carry

        lax.fori_loop(0, 2 * reps, tile, 0)
    arrive(experts - 1)

    flat = pl.ds(0, width)
    streams = [pl.ds(q * (width // 2), width // 2) for q in range(2)]
    first, second, third, last = {}, {}, {}, []

    def scatter_core(i):
        make_units(experts - 1, i, 0)
        project(i, 0)
        c = lax.rem(r + 1 + i, reps)
        first[i] = remote(
            x.at[c, :, :, other, :, flat], r1.at[i], rs_send.at[i, 0], rs_recv.at[i, 0], core_mate
        )

    def scatter_second(i):
        make_units(experts - 1, i, 1)
        first[i].wait_recv()
        project(i, 1)
        c = lax.rem(r + 1 + i, reps)
        for q, columns in enumerate(streams):
            if q == 0:
                src, mate = x.at[c, :, 1 - xs, core, :, columns], x_mate
            else:
                src, mate = x.at[c, 1 - ys, :, core, :, columns], y_mate
            second[i, q] = remote(
                src, r2.at[i, :, :, columns], rs_send.at[i, 1 + q], rs_recv.at[i, 1 + q], mate
            )

    def scatter_third(i):
        c = lax.rem(r + 1 + i, reps)
        for q, columns in enumerate(streams):
            second[i, q].wait_recv()

            def add(n, carry, q=q, columns=columns):
                at = pl.ds(pl.multiple_of(n * 16, 16), 16)
                for k in range(2):
                    where = (c, k, xs, core, at, columns) if q == 0 else (c, ys, k, core, at, columns)
                    total = x[where].astype(jnp.float32) + r2[i, k, at, columns].astype(jnp.float32)
                    x[where] = total.astype(jnp.bfloat16)
                return carry

            lax.fori_loop(0, rows // 16, add, 0)
            if q == 0:
                src, mate = x.at[c, 1 - ys, xs, core, :, columns], y_mate
            else:
                src, mate = x.at[c, ys, 1 - xs, core, :, columns], x_mate
            third[i, q] = remote(
                src, r3.at[i, :, columns], rs_send.at[i, 3 + q], rs_recv.at[i, 3 + q], mate
            )

    def scatter_rep(i):
        for q in range(2):
            third[i, q].wait_recv()
        c = lax.rem(r + 1 + i, reps)
        if i == reps - 1:
            return

        def add(n, carry):
            at = pl.ds(pl.multiple_of(n * 16, 16), 16)
            where = (c, ys, xs, core, at, flat)
            total = x[where].astype(jnp.float32) + r3[i, at, :].astype(jnp.float32)
            x[where] = total.astype(jnp.bfloat16)
            return carry

        lax.fori_loop(0, rows // 16, add, 0)
        last.append(
            remote(
                x.at[c, ys, xs, core, :, flat], rz.at[i], o_send.at[i], o_recv.at[i], rep_mates[i]
            )
        )

    for step in range(reps + 3):
        if step < reps:
            scatter_core(step)
        for lag, work in ((1, scatter_second), (2, scatter_third), (3, scatter_rep)):
            if 0 <= step - lag < reps:
                work(step - lag)
    for copy in last:
        copy.wait_recv()

    def finish(n, carry):
        at = pl.ds(pl.multiple_of(n * 16, 16), 16)
        total = x[r, ys, xs, core, at, flat].astype(jnp.float32)
        total = total + r3[reps - 1, at, :].astype(jnp.float32)
        for k in range(reps - 1):
            total = total + rz[k, at, :].astype(jnp.float32)
        out_ref[at, :] = total.astype(jnp.bfloat16)
        return carry

    lax.fori_loop(0, rows // 16, finish, 0)
    for copy in list(first.values()) + list(second.values()) + list(third.values()) + last:
        copy.wait_send()


def fused(tokens, weight, gate_up, down, reps):
    rows, width = tokens.shape
    experts, block_depth, columns = gate_up.shape
    part = columns // 2 // reps
    all_experts = weight.shape[1]
    high = lax.reduce_precision(weight, 8, 7)
    marks = jnp.concatenate([high, weight - high], axis=1).astype(jnp.bfloat16)
    marks = jnp.pad(marks, ((0, 0), (0, LANES - 2 * all_experts)))
    x = jnp.concatenate([tokens, marks], axis=1)
    lane = jnp.arange(LANES, dtype=jnp.int32)
    own = lax.axis_index("tok") * experts + jnp.arange(experts, dtype=jnp.int32)
    chosen = (lane[None, :] == own[:, None]) | (lane[None, :] == own[:, None] + all_experts)
    sel = jnp.broadcast_to(chosen[:, :, None], (experts, LANES, part)).astype(jnp.bfloat16)
    depth = block_depth * reps
    bf16 = jnp.bfloat16
    dma = pltpu.SemaphoreType.DMA
    hbm = pl.BlockSpec(memory_space=pl.ANY)
    vmem = pl.BlockSpec(memory_space=pltpu.VMEM)
    return pl.pallas_call(
        fused_kernel,
        out_shape=[
            jax.ShapeDtypeStruct((rows, width), bf16),
            jax.ShapeDtypeStruct(gate_up.shape, bf16),
        ],
        in_specs=[hbm, vmem, hbm, hbm],
        out_specs=[vmem, hbm],
        scratch_shapes=[
            pltpu.VMEM((reps, 2, 2, 2, rows, width + LANES), bf16),
            pltpu.VMEM((experts, depth, 2 * part), bf16),
            pltpu.VMEM((experts * part, width), bf16),
            pltpu.VMEM((reps, 2, 4 * rows, experts * part), bf16),
            pltpu.VMEM((reps, 2, 2, rows, width), bf16),
            pltpu.VMEM((reps, 2, rows, width), bf16),
            pltpu.VMEM((reps, rows, width), bf16),
            pltpu.VMEM((reps - 1, rows, width), bf16),
            pltpu.VMEM((2, 128, columns), jnp.float32),
            pltpu.VMEM((2, 128, columns), bf16),
            dma((2 + HALVES * experts,)),
            dma((2,)),
            dma((2,)),
            dma((experts, reps - 1, HALVES)),
            dma((experts, reps - 1, HALVES)),
            dma((reps - 1,)),
            dma((reps - 1,)),
            dma((reps, 3)),
            dma((reps, 3)),
            dma((reps, 5)),
            dma((reps, 5)),
            dma((reps - 1,)),
            dma((reps - 1,)),
        ],
        compiler_params=pltpu.CompilerParams(
            collective_id=0, has_side_effects=True, vmem_limit_bytes=62 << 20
        ),
    )(x, sel, gate_up, down.reshape(experts * part, width))[0]


def per_device(hidden_states, routes, gate_prob, gate_up, down):
    groups = lax.axis_size("tok")
    reps = lax.axis_size("rep")
    experts = gate_up.shape[0]
    _, token_count, width = hidden_states.shape
    part = gate_up.shape[2] // 2 // reps
    all_experts = groups * experts
    tokens = hidden_states[0]
    total_bytes = groups * reps * token_count * width * 2
    chunks = max(1, total_bytes // GATHER_BYTES)
    chunk = token_count // chunks

    hit = routes[0][:, :, None] == jnp.arange(all_experts, dtype=jnp.int32)
    weight = jnp.sum(jnp.where(hit, gate_prob[0][:, :, None], 0.0), axis=1)
    sizes = (groups, reps, experts, token_count, width, gate_up.shape[1:], down.shape[1])
    if sizes == (8, 4, 4, 128, 2048, (512, 2048), 256):
        return fused(tokens, weight, gate_up, down, reps)[None]
    gate, up = reshard_gate_up(gate_up, reps)
    stacked_down = down.astype(jnp.bfloat16).reshape(experts * part, width)
    first = lax.axis_index("tok") * experts

    def one_chunk(rows, row_weight):
        everyone = lax.all_gather(rows, ("rep", "tok"), axis=0, tiled=True)
        all_weight = lax.all_gather(row_weight, ("rep", "tok"), axis=0, tiled=True)
        mine = lax.dynamic_slice_in_dim(all_weight, first, experts, 1)
        scale = jnp.repeat(mine, part, axis=1)
        g = jnp.dot(everyone, gate, preferred_element_type=jnp.float32)
        u = jnp.dot(everyone, up, preferred_element_type=jnp.float32)
        units = (jax.nn.silu(g) * u * scale).astype(jnp.bfloat16)
        partial = jnp.dot(units, stacked_down, preferred_element_type=jnp.float32)
        return lax.psum_scatter(
            partial.astype(jnp.bfloat16), ("rep", "tok"), scatter_dimension=0, tiled=True
        )

    if chunks == 1:
        return one_chunk(tokens, weight)[None]
    mixed = lax.map(
        lambda part_of: one_chunk(*part_of),
        (tokens.reshape(chunks, chunk, width), weight.reshape(chunks, chunk, all_experts)),
    )
    return mixed.reshape(1, token_count, width)


def solution(mesh):
    return jax.shard_map(
        per_device,
        mesh=mesh,
        in_specs=(
            P("rep", "tok", None),
            P("rep", "tok", None),
            P("rep", "tok", None),
            P("tok", "rep", None),
            P("tok", "rep", None),
        ),
        out_specs=P("rep", "tok", None),
        check_vma=False,
    )
```
